256 devices in a mesh: row: 16 (over z_hi, y, core), col: 16 (over x, z_lo).
Axes of the slice: x: 4, y: 4, z: 8 (z_hi: 2, z_lo: 4; z = z_hi * 4 + z_lo), core: 2. Of those that a mesh axis runs over, the one named last changes fastest.
Arguments:
- vectors: float32 [32, 1, 16, 16, 256], P(None, None, 'row', 'col'), may hold values from -6 to 6
- tiles: bfloat16 [16, 16, 80, 256, 256], P('row', 'col'), may hold values from -0.0390625 to 0.0390625
- pattern: int32 [16, 16, 80, 2], P('row', 'col'), may hold values from -1 to 255, as said below
Outputs:
- filtered: float32 [32, 1, 16, 16, 256], P(None, None, 'row', 'col')
The draws below stay inside these ranges and needn't reach their ends.
Inputs may be any that keep to these rules, and one draw needn't show every extreme that they name: pattern[r, c, s] = (i, j) with i <= j, (i // 16) % 16 == r and j % 16 == c, or (-1, -1) for an empty slot. Live slots come first in each grid position's list, and some grid position has all 80 slots live. A pair may occur more than once; its tiles then add.
All inputs are finite; a program needn't handle non-finite values.
Results may differ from the reference program's by a relative error of at most 0.0085.
Values may be sent and summed in bfloat16 or wider, within the bound.
A program may use at most 64 MiB of HBM per device.

```python
import jax
import jax.numpy as jnp
from jax import lax

BS = 256
VEC = 32
BLK_DEV = 1
TILES_DEV = 80
DEG = 5
NBLK = 256
N_ROW = 16
N_COL = 16


def draw_pattern(key, part):
    key = jax.random.fold_in(key, 11)
    key_row, key_col, key_count, key_full = jax.random.split(key, 4)
    shape = (N_ROW, N_COL, TILES_DEV)
    row_ids = jnp.arange(N_ROW, dtype=jnp.int32).reshape(N_ROW, 1, 1)
    col_ids = jnp.arange(N_COL, dtype=jnp.int32).reshape(1, N_COL, 1)
    total_blocks = BLK_DEV * N_ROW * N_COL
    picked = jax.random.randint(key_row, shape, 0, BLK_DEV * N_COL, dtype=jnp.int32)
    block_row = (picked // N_COL * N_ROW + row_ids) * N_COL + picked % N_COL
    block_row = jnp.minimum(block_row, total_blocks - N_COL + col_ids)
    lowest = (block_row - col_ids + N_COL - 1) // N_COL
    span = total_blocks // N_COL - lowest
    raw = jax.random.randint(key_col, shape, 0, 2 ** 30, dtype=jnp.int32)
    block_col = (lowest + raw % span) * N_COL + col_ids
    counts = jax.random.randint(key_count, (N_ROW, N_COL), TILES_DEV // 6, TILES_DEV + 1, dtype=jnp.int32)
    full_pick = jax.random.randint(key_full, (), 0, N_ROW * N_COL, dtype=jnp.int32)
    grid_ids = jnp.arange(N_ROW * N_COL, dtype=jnp.int32).reshape(N_ROW, N_COL)
    counts = jnp.where(grid_ids == full_pick, TILES_DEV, counts)
    live_slots = jnp.arange(TILES_DEV, dtype=jnp.int32).reshape(1, 1, TILES_DEV) < counts[:, :, None]
    block_row = jnp.where(live_slots, block_row, -1)
    block_col = jnp.where(live_slots, block_col, -1)
    return jnp.stack([block_row, block_col], axis=-1).astype(jnp.int32)


def shard_levels(key, shape, pieces, least, high):
    def one(dim, blocks):
        steps = jax.random.uniform(jax.random.fold_in(jax.random.fold_in(key, 6), dim), (blocks,), jnp.float32, least / len(pieces), high / len(pieces))
        return jnp.repeat(jnp.exp(steps), shape[dim] // blocks).reshape((-1,) + (1,) * (len(shape) - dim - 1))

    gain = one(*pieces[0])
    for cut in pieces[1:]:
        gain = gain * one(*cut)
    return gain


def centred(key, shape, spread, most, shards=(), held_as=jnp.bfloat16):
    array = spread * jax.random.normal(key, shape, jnp.float32)
    if shards:
        array = array * shard_levels(key, shape, shards, -0.22, 0.18)
    return jnp.clip(array, -most, most).astype(held_as)


def setup_inputs(seed: int = 0) -> dict:
    splits = jax.random.split(jax.random.key(seed), 4)
    return {
        "vectors": centred(splits[0], (VEC, BLK_DEV, N_ROW, N_COL, BS), 1.0, 6.0, ((2, 16), (3, 16)), jnp.float32),
        "tiles": centred(splits[1], (N_ROW, N_COL, TILES_DEV, BS, BS), (BS * TILES_DEV // BLK_DEV) ** -0.5, 0.0390625, ((0, 16), (1, 16))),
        "pattern": draw_pattern(jax.random.fold_in(splits[3], 71), 0),
    }


CENTER = 0.5
HALF_WIDTH = 3.0


def apply_matrix(blocks, tile_list, slot_list):
    def one_device(accum, item):
        tile_set, slot_pairs = item
        live_slots = slot_pairs[:, 0] >= 0
        block_row = jnp.where(live_slots, slot_pairs[:, 0], 0).astype(jnp.int32)
        block_col = jnp.where(live_slots, slot_pairs[:, 1], 0).astype(jnp.int32)
        weight_mask = live_slots.astype(jnp.float32)[:, None, None]
        tile_float = tile_set.astype(jnp.float32)
        col_inputs = blocks[block_col].astype(jnp.float32)
        row_inputs = blocks[block_row].astype(jnp.float32)
        forward_terms = jnp.einsum('svb,sab->sva', col_inputs, tile_float) * weight_mask
        mirror_terms = jnp.einsum('sva,sab->svb', row_inputs, tile_float) * weight_mask
        accum = accum.at[block_row].add(forward_terms).at[block_col].add(mirror_terms)
        return accum, None

    start_sum = jnp.zeros((NBLK, VEC, BS), jnp.float32)
    result, _ = lax.scan(one_device, start_sum, (tile_list, slot_list))
    return result


def reference(vectors, tiles, pattern):
    present = jnp.transpose(vectors, (1, 2, 3, 0, 4)).reshape(NBLK, VEC, BS)
    tile_list = tiles.reshape(N_ROW * N_COL, TILES_DEV, BS, BS)
    slot_list = pattern.reshape(N_ROW * N_COL, TILES_DEV, 2)
    previous = present
    for term_index in range(DEG):
        product = apply_matrix(present.astype(jnp.bfloat16), tile_list, slot_list)
        scaled = (product - CENTER * present) / HALF_WIDTH
        if term_index == 0:
            following = scaled
        else:
            following = 2.0 * scaled - previous
        previous, present = present, following
    shaped = present.reshape(BLK_DEV, N_ROW, N_COL, VEC, BS)
    return jnp.transpose(shaped, (3, 0, 1, 2, 4))
```

```python
import functools

import jax
import jax.numpy as jnp
from jax import lax
from jax.experimental import pallas as pl
from jax.experimental.pallas import tpu as pltpu
from jax.sharding import PartitionSpec as P

MESH = pl.DeviceIdType.MESH
DEG = 5
CENTER = 0.5
HALF_WIDTH = 3.0
GROUP = 16
SLOTS = 80
VEC = 32
BS = 256
HB = 128
LOADS = 8

COL_STEPS = [(dx, dz) for dx in range(4) for dz in range(4) if dx or dz]
PAIR_STEPS = [(dy, dk) for dy in range(4) for dk in range(2) if dy or dk]


def kernel(
    meta, vec, tiles_hbm, out,
    tiles, flipped, run_m, run_f, now, before,
    yc_0, yc_1, yr, rows, send_m, recv_m, send_z, recv_z, send_f, recv_f,
    load_sem,
    yc_send, yc_recv, yr_send, yr_recv, yz_send, yz_recv, yf_send, yf_recv,
    m_send, m_recv, z_send, z_recv, f_send, f_recv,
):
    row, col = lax.axis_index("row"), lax.axis_index("col")
    half = row // 8
    pair = row % 8
    yc = (yc_0, yc_1)
    y, core = pair // 2, pair % 2
    x, z = col // 4, col % 4
    other = (1 - half) * 8

    col_ids = [((x + dx) % 4) * 4 + (z + dz) % 4 for dx, dz in COL_STEPS]
    pair_ids = [((y + dy) % 4) * 2 + (core + dk) % 2 for dy, dk in PAIR_STEPS]
    far = other + pair

    def remote(src, dst, send, recv, to):
        return pltpu.make_async_remote_copy(
            src_ref=src, dst_ref=dst, send_sem=send, recv_sem=recv,
            device_id=to, device_id_type=MESH,
        )

    def take(ref, sem):
        pltpu.make_async_copy(ref, ref, sem).wait()

    def load(n):
        rows = pl.ds(n * (SLOTS // LOADS), SLOTS // LOADS)
        return pltpu.make_async_copy(tiles_hbm.at[rows], tiles.at[rows], load_sem.at[n])

    for n in range(LOADS):
        load(n).start()

    barrier = pltpu.get_barrier_semaphore()
    for c in col_ids:
        pl.semaphore_signal(barrier, inc=1, device_id=(row, c), device_id_type=MESH)
    for p in pair_ids:
        pl.semaphore_signal(barrier, inc=1, device_id=(half * 8 + p, col), device_id_type=MESH)
    pl.semaphore_signal(barrier, inc=1, device_id=(far, col), device_id_type=MESH)

    now[...] = vec[...]
    before[...] = vec[...]
    run_m[0, SLOTS] = jnp.zeros((VEC, BS), jnp.float32)
    run_m[1, SLOTS] = jnp.zeros((VEC, BS), jnp.float32)
    run_f[0, SLOTS] = jnp.zeros((VEC, HB), jnp.float32)
    run_f[1, SLOTS] = jnp.zeros((VEC, HB), jnp.float32)

    def place(par, h):
        block = now[:, h * HB : (h + 1) * HB].astype(jnp.bfloat16)
        yc[h][col] = block
        yr[par, row, h] = block

    def spread_col(h):
        for c in col_ids:
            remote(yc[h].at[col], yc[h].at[col], yc_send.at[h], yc_recv.at[h], (row, c)).start()

    def spread_row(par):
        mine = yr.at[par, row]
        remote(mine, mine, yz_send.at[par], yz_recv.at[par], (far, col)).start()
        for p in pair_ids:
            remote(mine, mine, yr_send.at[par], yr_recv.at[par], (half * 8 + p, col)).start()

    place(0, 0)
    place(0, 1)
    pl.semaphore_wait(barrier, len(col_ids) + len(pair_ids) + 1)
    spread_col(0)
    spread_col(1)
    spread_row(0)

    for n in range(LOADS):
        load(n).wait()

        def flip(s, carry):
            flipped[s] = tiles[s].T
            return carry

        lax.fori_loop(n * (SLOTS // LOADS), (n + 1) * (SLOTS // LOADS), flip, 0, unroll=True)

    def mirror(h):
        total = None
        for p in range(SLOTS):
            s, b = meta[0, p], meta[1, p]
            term = jnp.dot(
                yc[h][b], tiles[s, h * HB : (h + 1) * HB, :], preferred_element_type=jnp.float32
            )
            total = term if p == 0 else jnp.where(meta[2, p] == 1, term, total + term)
            run_m[h, p] = total

    def forward(h):
        total = None
        for p in range(SLOTS):
            s, b = meta[4, p], meta[5, p]
            term = jnp.dot(
                rows[b], flipped[s, :, h * HB : (h + 1) * HB], preferred_element_type=jnp.float32
            )
            total = term if p == 0 else jnp.where(meta[6, p] == 1, term, total + term)
            run_f[h, p] = total

    def mirror_block(r):
        last = meta[3, r]
        return (run_m[0, last] + run_m[1, last]).astype(jnp.bfloat16)

    def step(t, carry):
        par = lax.rem(t, 2)

        take(yr.at[par, 0], yz_recv.at[par])
        theirs = yr.at[par, far]
        for p in pair_ids:
            remote(theirs, theirs, yf_send.at[par], yf_recv.at[par], (half * 8 + p, col)).start()

        take(yc[0].at[pl.ds(0, 15)], yc_recv.at[0])
        mirror(0)
        take(yc[1].at[pl.ds(0, 15)], yc_recv.at[1])
        mirror(1)

        for q, base in ((0, other), (1, half * 8)):
            block = mirror_block(base + pair)
            recv_m[par, q, pair, 0] = block[:, :HB]
            recv_m[par, q, pair, 1] = block[:, HB:]
            for n, p in enumerate(pair_ids):
                block = mirror_block(base + p)
                send_m[q, n, 0] = block[:, :HB]
                send_m[q, n, 1] = block[:, HB:]
                remote(
                    send_m.at[q, n], recv_m.at[par, q, pair], m_send.at[q], m_recv.at[par, q],
                    (half * 8 + p, col),
                ).start()

        take(yr.at[par, pl.ds(0, 7)], yr_recv.at[par])
        take(yr.at[par, pl.ds(0, 7)], yf_recv.at[par])
        for r in range(GROUP):
            rows[r, :, :HB] = yr[par, r, 0]
            rows[r, :, HB:] = yr[par, r, 1]
        for h in range(2):
            forward(h)
            recv_f[h, col] = run_f[h, meta[7, col]].astype(jnp.bfloat16)
            for n, c in enumerate(col_ids):
                send_f[h, n] = run_f[h, meta[7, c]].astype(jnp.bfloat16)
                remote(
                    send_f.at[h, n], recv_f.at[h, col], f_send.at[h], f_recv.at[h], (row, c)
                ).start()

        take(recv_m.at[par, 0, pl.ds(0, 7)], m_recv.at[par, 0])
        for h in range(2):
            part = recv_m[par, 0, 0, h].astype(jnp.float32)
            for n in range(1, 8):
                part = part + recv_m[par, 0, n, h].astype(jnp.float32)
            send_z[h] = part.astype(jnp.bfloat16)
        remote(send_z, recv_z.at[par], z_send, z_recv.at[par], (far, col)).start()

        take(recv_m.at[par, 1, pl.ds(0, 7)], m_recv.at[par, 1])
        take(yr.at[par, 0], yz_send.at[par])
        take(yr.at[par, pl.ds(0, 7)], yr_send.at[par])
        take(yr.at[par, pl.ds(0, 7)], yf_send.at[par])
        take(recv_z.at[par], z_recv.at[par])
        scale = jnp.where(t == 0, 1.0, 2.0).astype(jnp.float32)
        keep = jnp.where(t == 0, 0.0, 1.0).astype(jnp.float32)
        for h in range(2):
            cut = slice(h * HB, (h + 1) * HB)
            take(recv_f.at[h, pl.ds(0, 15)], f_recv.at[h])
            take(yc[h].at[pl.ds(0, 15)], yc_send.at[h])
            total = recv_z[par, h].astype(jnp.float32)
            for n in range(8):
                total = total + recv_m[par, 1, n, h].astype(jnp.float32)
            for n in range(GROUP):
                total = total + recv_f[h, n].astype(jnp.float32)
            present = now[:, cut]
            scaled = (total - CENTER * present) * (1.0 / HALF_WIDTH)
            following = scale * scaled - keep * before[:, cut]
            before[:, cut] = present
            now[:, cut] = following

            @pl.when(t < DEG - 1)
            def _():
                place(1 - par, h)
                spread_col(h)

        @pl.when(t < DEG - 1)
        def _():
            spread_row(1 - par)

        for h in range(2):
            take(send_f.at[h], f_send.at[h])
            take(send_m.at[h], m_send.at[h])
        take(send_z, z_send)
        return carry

    lax.fori_loop(0, DEG, step, 0)
    out[...] = now[...]


def ordered(key, block):
    slots = jnp.arange(SLOTS, dtype=jnp.int32)
    ahead = (key[None, :] < key[:, None]) | (
        (key[None, :] == key[:, None]) & (slots[None, :] < slots[:, None])
    )
    rank = jnp.sum(ahead, axis=1, dtype=jnp.int32)
    chosen = rank[None, :] == slots[:, None]
    slot = jnp.sum(jnp.where(chosen, slots[None, :], 0), axis=1, dtype=jnp.int32)
    source = jnp.sum(jnp.where(chosen, block[None, :], 0), axis=1, dtype=jnp.int32)
    group = jnp.sum(jnp.where(chosen, key[None, :], 0), axis=1, dtype=jnp.int32)
    start = jnp.concatenate([jnp.ones((1,), jnp.int32), (group[1:] != group[:-1]).astype(jnp.int32)])
    classes = jnp.arange(GROUP, dtype=jnp.int32)[:, None]
    upto = jnp.sum(key[None, :] <= classes, axis=1, dtype=jnp.int32)
    some = jnp.any(key[None, :] == classes, axis=1)
    last = jnp.where(some, upto - 1, SLOTS)
    pad = lambda a: jnp.pad(a, (0, 128 - a.shape[0]))
    return [pad(slot), pad(source), pad(start), pad(last)]


def per_device(vectors, tiles, pattern):
    slot_pairs = pattern[0, 0]
    live = slot_pairs[:, 0] >= 0
    row_key = jnp.where(live, slot_pairs[:, 0] % GROUP, GROUP)
    col_key = jnp.where(live, slot_pairs[:, 1] // GROUP, GROUP)
    row_block = jnp.where(live, row_key, 0)
    col_block = jnp.where(live, col_key, 0)
    meta = jnp.stack(ordered(col_key, row_block) + ordered(row_key, col_block))

    half16 = (VEC, HB)
    dma = pltpu.SemaphoreType.DMA
    filtered = pl.pallas_call(
        kernel,
        out_shape=jax.ShapeDtypeStruct((VEC, BS), jnp.float32),
        in_specs=[
            pl.BlockSpec(memory_space=pltpu.SMEM),
            pl.BlockSpec(memory_space=pltpu.VMEM),
            pl.BlockSpec(memory_space=pl.ANY),
        ],
        out_specs=pl.BlockSpec(memory_space=pltpu.VMEM),
        scratch_shapes=[
            pltpu.VMEM((SLOTS, BS, BS), jnp.bfloat16),
            pltpu.VMEM((SLOTS, BS, BS), jnp.bfloat16),
            pltpu.VMEM((2, SLOTS + 1, VEC, BS), jnp.float32),
            pltpu.VMEM((2, SLOTS + 1, VEC, HB), jnp.float32),
            pltpu.VMEM((VEC, BS), jnp.float32),
            pltpu.VMEM((VEC, BS), jnp.float32),
            pltpu.VMEM((GROUP,) + half16, jnp.bfloat16),
            pltpu.VMEM((GROUP,) + half16, jnp.bfloat16),
            pltpu.VMEM((2, GROUP, 2) + half16, jnp.bfloat16),
            pltpu.VMEM((GROUP, VEC, BS), jnp.bfloat16),
            pltpu.VMEM((2, 7, 2) + half16, jnp.bfloat16),
            pltpu.VMEM((2, 2, 8, 2) + half16, jnp.bfloat16),
            pltpu.VMEM((2,) + half16, jnp.bfloat16),
            pltpu.VMEM((2, 2) + half16, jnp.bfloat16),
            pltpu.VMEM((2, 15) + half16, jnp.bfloat16),
            pltpu.VMEM((2, GROUP) + half16, jnp.bfloat16),
            dma((LOADS,)),
            dma((2,)), dma((2,)), dma((2,)), dma((2,)), dma((2,)), dma((2,)), dma((2,)), dma((2,)),
            dma((2,)), dma((2, 2)), dma, dma((2,)), dma((2,)), dma((2,)),
        ],
        compiler_params=pltpu.CompilerParams(
            collective_id=0, has_side_effects=True, vmem_limit_bytes=48 * 2**20
        ),
        cost_estimate=pl.CostEstimate(
            flops=DEG * 4 * SLOTS * VEC * BS * BS, bytes_accessed=SLOTS * BS * BS * 2, transcendentals=0
        ),
        name="chebyshev",
    )(meta, vectors.reshape(VEC, BS), tiles.reshape(SLOTS, BS, BS))
    return filtered.reshape(VEC, 1, 1, 1, BS)


def solution(mesh):
    placed = (
        P(None, None, "row", "col", None),
        P("row", "col", None, None, None),
        P("row", "col", None, None),
    )
    return jax.shard_map(
        per_device,
        mesh=mesh,
        in_specs=placed,
        out_specs=P(None, None, "row", "col", None),
        check_vma=False,
    )
```

```python
import functools

import jax
import jax.numpy as jnp
from jax import lax
from jax.experimental import pallas as pl
from jax.experimental.pallas import tpu as pltpu
from jax.sharding import PartitionSpec as P

MESH = pl.DeviceIdType.MESH
DEG = 5
CENTER = 0.5
HALF_WIDTH = 3.0
GROUP = 16
SLOTS = 80
VEC = 32
BS = 256
HB = 128
LOADS = 8

PAIR_STEPS = [(dy, dk) for dy in (2, 1, 3, 0) for dk in range(2) if dy or dk]


def kernel(
    vec, pattern, tiles_hbm, out,
    tiles, flipped, run_m, run_f, now, before, table, meta,
    yc, yr, rows, send_m, recv_m, send_z, recv_z, send_x, recv_x, send_w, recv_w, gathered,
    load_sem, meta_sem,
    cz_send, cz_recv, cx_send, cx_recv, yr_send, yr_recv, yz_send, yz_recv, yf_send, yf_recv,
    m_send, m_recv, z_send, z_recv, x_send, x_recv, w_send, w_recv,
):
    row, col = lax.axis_index("row"), lax.axis_index("col")
    half = row // 8
    pair = row % 8
    y, core = pair // 2, pair % 2
    x, z = col // 4, col % 4
    other = (1 - half) * 8
    far = other + pair

    z_near = [z + 1 - 2 * (z % 2), (z + 2) % 4, 3 - z]
    x_near = [(x + 2) % 4, (x + 1) % 4, (x + 3) % 4]
    pair_ids = [((y + dy) % 4) * 2 + (core + dk) % 2 for dy, dk in PAIR_STEPS]

    def remote(src, dst, send, recv, to):
        return pltpu.make_async_remote_copy(
            src_ref=src, dst_ref=dst, send_sem=send, recv_sem=recv,
            device_id=to, device_id_type=MESH,
        )

    def take(ref, sem):
        pltpu.make_async_copy(ref, ref, sem).wait()

    def load(n):
        part = pl.ds(n * (SLOTS // LOADS), SLOTS // LOADS)
        return pltpu.make_async_copy(tiles_hbm.at[part], tiles.at[part], load_sem.at[n])

    barrier = pltpu.get_barrier_semaphore()
    greeted = [(far, col)]
    greeted += [(row, x * 4 + b) for b in z_near]
    greeted += [(row, a * 4 + z) for a in x_near]
    greeted += [(half * 8 + p, col) for p in pair_ids]
    for to in greeted:
        pl.semaphore_signal(barrier, inc=1, device_id=to, device_id_type=MESH)

    for n in range(LOADS):
        load(n).start()

    for h in range(2):
        block = vec[pl.ds(h, VEC, stride=2), :]
        now[h] = block
        before[h] = block
        run_m[h, SLOTS] = jnp.zeros((VEC, BS), jnp.float32)
        run_f[h, SLOTS] = jnp.zeros((VEC, HB), jnp.float32)

    def place(par):
        block = jnp.concatenate([now[0], now[1]], axis=1).astype(jnp.bfloat16)
        yc[col] = block
        yr[par, row] = block

    def spread(par):
        mine = yr.at[par, row]
        remote(mine, mine, yz_send.at[par], yz_recv.at[par], (far, col)).start()
        mine = yc.at[col]
        for n, b in enumerate(z_near):
            remote(mine, mine, cz_send, cz_recv.at[n], (row, x * 4 + b)).start()
        for a in x_near:
            remote(mine, mine, cx_send, cx_recv, (row, a * 4 + z)).start()
        mine = yr.at[par, row]
        for p in pair_ids:
            remote(mine, mine, yr_send.at[par], yr_recv.at[par], (half * 8 + p, col)).start()

    place(0)
    pl.semaphore_wait(barrier, len(greeted))
    spread(0)

    table[...] = jnp.full((8, 128), -1, jnp.int32)
    table[0:2, 0:SLOTS] = pattern[...]
    ids = table[...]
    live = ids >= 0
    keys = jnp.where(live, jnp.concatenate([ids[0:1] % GROUP, ids[1:2] // GROUP, ids[2:8]], axis=0), GROUP)
    down = lax.broadcasted_iota(jnp.int32, (128, 128), 0)
    along = lax.broadcasted_iota(jnp.int32, (128, 128), 1)

    def across(line):
        return jnp.broadcast_to(line, (128, 128))

    row_across, col_across = across(keys[0:1]), across(keys[1:2])
    row_down, col_down = row_across.T, col_across.T

    def count(mask, value=1):
        return jnp.sum(jnp.where(mask, value, 0), axis=0, keepdims=True)

    lines = []
    for key, key_down, source_down in (
        (col_across, col_down, row_down), (row_across, row_down, col_down)
    ):
        rank = count((key_down < key) | ((key_down == key) & (down < along)))
        chosen = across(rank).T == along
        group = count(chosen, key_down)
        lines.append(count(chosen, down))
        lines.append(count(chosen & (source_down < GROUP), source_down))
        lines.append((group != pltpu.roll(group, 1, 1)).astype(jnp.int32))
        lines.append(jnp.where(count(key_down == along) > 0, count(key_down <= along) - 1, SLOTS))
    for n, line in enumerate(lines):
        table[n : n + 1, :] = line
    tell = pltpu.make_async_copy(table, meta, meta_sem)
    tell.start()

    def flip_all():
        for n in range(LOADS):
            load(n).wait()

            def flip(s, carry):
                flipped[s] = tiles[s].T
                return carry

            lax.fori_loop(n * (SLOTS // LOADS), (n + 1) * (SLOTS // LOADS), flip, 0, unroll=True)
        tell.wait()

    def mirror(h):
        total = None
        for p in range(SLOTS):
            s, b = meta[0, p], meta[1, p]
            cut = slice(h * HB, (h + 1) * HB)
            term = jnp.dot(yc[b, :, cut], tiles[s, cut, :], preferred_element_type=jnp.float32)
            total = term if p == 0 else jnp.where(meta[2, p] == 1, term, total + term)
            run_m[h, p] = total

    def forward(h):
        total = None
        for p in range(SLOTS):
            s, b = meta[4, p], meta[5, p]
            cut = slice(h * HB, (h + 1) * HB)
            term = jnp.dot(rows[b], flipped[s, :, cut], preferred_element_type=jnp.float32)
            total = term if p == 0 else jnp.where(meta[6, p] == 1, term, total + term)
            run_f[h, p] = total

    def mirror_block(r):
        last = meta[3, r]
        return (run_m[0, last] + run_m[1, last]).astype(jnp.bfloat16)

    def forward_block(h, c):
        return run_f[h, meta[7, c]].astype(jnp.bfloat16)

    def step(t, carry):
        par = lax.rem(t, 2)

        for n, b in enumerate(z_near):
            theirs = yc.at[x * 4 + b]
            take(theirs, cz_recv.at[n])
            for a in x_near:
                remote(theirs, theirs, cx_send, cx_recv, (row, a * 4 + z)).start()
        theirs = yr.at[par, far]
        take(theirs, yz_recv.at[par])
        for p in pair_ids:
            remote(theirs, theirs, yf_send.at[par], yf_recv.at[par], (half * 8 + p, col)).start()

        @pl.when(t == 0)
        def _():
            flip_all()

        take(yc.at[pl.ds(0, 12)], cx_recv)
        mirror(0)
        mirror(1)

        for q, base in ((0, other), (1, half * 8)):
            for n, p in enumerate(pair_ids):
                send_m[q, n] = mirror_block(base + p)
                remote(
                    send_m.at[q, n], recv_m.at[par, q, pair], m_send.at[q], m_recv.at[par, q],
                    (half * 8 + p, col),
                ).start()
            recv_m[par, q, pair] = mirror_block(base + pair)

        take(yc.at[pl.ds(0, 12)], cx_send)
        take(yc.at[pl.ds(0, 3)], cz_send)
        take(yr.at[par, pl.ds(0, 7)], yr_recv.at[par])
        take(yr.at[par, pl.ds(0, 7)], yf_recv.at[par])
        for r in range(GROUP):
            rows[r] = yr[par, r]
        for h in range(2):
            forward(h)
            for n, a in enumerate(x_near):
                for b in range(4):
                    send_x[h, n, b] = forward_block(h, a * 4 + b)
                remote(
                    send_x.at[h, n], recv_x.at[h, x], x_send.at[h], x_recv.at[h], (row, a * 4 + z)
                ).start()
            for b in range(4):
                recv_x[h, x, b] = forward_block(h, x * 4 + b)

        take(recv_m.at[par, 0, pl.ds(0, 7)], m_recv.at[par, 0])
        part = recv_m[par, 0, 0].astype(jnp.float32)
        for n in range(1, 8):
            part = part + recv_m[par, 0, n].astype(jnp.float32)
        send_z[...] = part.astype(jnp.bfloat16)
        remote(send_z, recv_z.at[par], z_send, z_recv.at[par], (far, col)).start()

        for h in range(2):
            take(recv_x.at[h, pl.ds(0, 3)], x_recv.at[h])
            for n, b in enumerate(z_near + [z]):
                part = recv_x[h, 0, b].astype(jnp.float32)
                for a in range(1, 4):
                    part = part + recv_x[h, a, b].astype(jnp.float32)
                if n < 3:
                    send_w[h, n] = part.astype(jnp.bfloat16)
                    remote(
                        send_w.at[h, n], recv_w.at[h, z], w_send.at[h], w_recv.at[h], (row, x * 4 + b)
                    ).start()
                else:
                    recv_w[h, z] = part.astype(jnp.bfloat16)

        take(recv_m.at[par, 1, pl.ds(0, 7)], m_recv.at[par, 1])
        part = recv_m[par, 1, 0].astype(jnp.float32)
        for n in range(1, 8):
            part = part + recv_m[par, 1, n].astype(jnp.float32)
        gathered[...] = part

        take(yr.at[par, 0], yz_send.at[par])
        take(yr.at[par, pl.ds(0, 7)], yr_send.at[par])
        take(yr.at[par, pl.ds(0, 7)], yf_send.at[par])
        take(recv_z.at[par], z_recv.at[par])
        gathered[...] += recv_z[par].astype(jnp.float32)
        scale = jnp.where(t == 0, 1.0, 2.0).astype(jnp.float32)
        keep = jnp.where(t == 0, 0.0, 1.0).astype(jnp.float32)
        for h in range(2):
            take(recv_w.at[h, pl.ds(0, 3)], w_recv.at[h])
            total = gathered[:, h * HB : (h + 1) * HB]
            for b in range(4):
                total = total + recv_w[h, b].astype(jnp.float32)
            present = now[h]
            scaled = (total - CENTER * present) * (1.0 / HALF_WIDTH)
            following = scale * scaled - keep * before[h]
            before[h] = present
            now[h] = following

        @pl.when(t < DEG - 1)
        def _():
            place(1 - par)
            spread(1 - par)

        for h in range(2):
            take(send_x.at[h], x_send.at[h])
            take(send_w.at[h], w_send.at[h])
            take(send_m.at[h], m_send.at[h])
        take(send_z, z_send)
        return carry

    lax.fori_loop(0, DEG, step, 0)
    for h in range(2):
        out[pl.ds(h, VEC, stride=2), :] = now[h]


def per_device(vectors, tiles, pattern):
    bf16, f32 = jnp.bfloat16, jnp.float32
    dma = pltpu.SemaphoreType.DMA
    vmem = pltpu.VMEM
    filtered = pl.pallas_call(
        kernel,
        out_shape=jax.ShapeDtypeStruct((VEC * 2, HB), f32),
        in_specs=[
            pl.BlockSpec(memory_space=pltpu.VMEM),
            pl.BlockSpec(memory_space=pltpu.VMEM),
            pl.BlockSpec(memory_space=pl.ANY),
        ],
        out_specs=pl.BlockSpec(memory_space=pltpu.VMEM),
        scratch_shapes=[
            vmem((SLOTS, BS, BS), bf16),
            vmem((SLOTS, BS, BS), bf16),
            vmem((2, SLOTS + 1, VEC, BS), f32),
            vmem((2, SLOTS + 1, VEC, HB), f32),
            vmem((2, VEC, HB), f32),
            vmem((2, VEC, HB), f32),
            vmem((8, 128), jnp.int32),
            pltpu.SMEM((8, 128), jnp.int32),
            vmem((GROUP, VEC, BS), bf16),
            vmem((2, GROUP, VEC, BS), bf16),
            vmem((GROUP, VEC, BS), bf16),
            vmem((2, 7, VEC, BS), bf16),
            vmem((2, 2, 8, VEC, BS), bf16),
            vmem((VEC, BS), bf16),
            vmem((2, VEC, BS), bf16),
            vmem((2, 3, 4, VEC, HB), bf16),
            vmem((2, 4, 4, VEC, HB), bf16),
            vmem((2, 3, VEC, HB), bf16),
            vmem((2, 4, VEC, HB), bf16),
            vmem((VEC, BS), f32),
            dma((LOADS,)), dma,
            dma, dma((3,)), dma, dma, dma((2,)), dma((2,)), dma((2,)), dma((2,)), dma((2,)), dma((2,)),
            dma((2,)), dma((2, 2)), dma, dma((2,)), dma((2,)), dma((2,)), dma((2,)), dma((2,)),
        ],
        compiler_params=pltpu.CompilerParams(
            collective_id=0, has_side_effects=True, vmem_limit_bytes=48 * 2**20
        ),
        cost_estimate=pl.CostEstimate(
            flops=DEG * 4 * SLOTS * VEC * BS * BS, bytes_accessed=SLOTS * BS * BS * 2, transcendentals=0
        ),
        name="chebyshev",
    )(vectors.reshape(VEC * 2, HB), pattern[0, 0].T, tiles.reshape(SLOTS, BS, BS))
    return filtered.reshape(VEC, 1, 1, 1, BS)


def solution(mesh):
    placed = (
        P(None, None, "row", "col", None),
        P("row", "col", None, None, None),
        P("row", "col", None, None),
    )
    return jax.shard_map(
        per_device,
        mesh=mesh,
        in_specs=placed,
        out_specs=P(None, None, "row", "col", None),
        check_vma=False,
    )
```

```python
import functools

import jax
import jax.numpy as jnp
from jax import lax
from jax.experimental import pallas as pl
from jax.experimental.pallas import tpu as pltpu
from jax.sharding import PartitionSpec as P

MESH = pl.DeviceIdType.MESH
DEG = 5
CENTER = 0.5
HALF_WIDTH = 3.0
GROUP = 16
SLOTS = 80
VEC = 32
BS = 256
HB = 128
LOADS = 8

PAIR_STEPS = [(dy, dk) for dy in (2, 1, 3, 0) for dk in range(2) if dy or dk]


def kernel(
    vec_hbm, pattern_hbm, tiles_hbm, out,
    vec, pattern,
    tiles, flipped, run_m, run_f, now, before, table, meta,
    yc_0, yc_1, yr, rows, send_m, recv_m, send_z, recv_z, send_x, recv_x, send_w, recv_w, recv_d, recv_e, gathered,
    load_sem, meta_sem, in_sem,
    cz_send, cz_recv, cx_send, cx_recv, yr_send, yr_recv, yz_send, yz_recv, yf_send, yf_recv,
    m_send, m_recv, z_send, z_recv, x_send, x_recv, w_send, w_recv, d_recv, e_recv,
):
    row, col = lax.axis_index("row"), lax.axis_index("col")
    yc = (yc_0, yc_1)
    half = row // 8
    pair = row % 8
    y, core = pair // 2, pair % 2
    x, z = col // 4, col % 4
    other = (1 - half) * 8
    far = other + pair

    z_near = [3 - z, (z + 2) % 4, z + 1 - 2 * (z % 2)]
    edge, inner = z % 3 == 0, z % 3 != 0
    upper, lower = half == 0, half == 1
    x_near = [(x + 2) % 4, (x + 1) % 4, (x + 3) % 4]
    pair_ids = [((y + dy) % 4) * 2 + (core + dk) % 2 for dy, dk in PAIR_STEPS]

    def remote(src, dst, send, recv, to):
        return pltpu.make_async_remote_copy(
            src_ref=src, dst_ref=dst, send_sem=send, recv_sem=recv,
            device_id=to, device_id_type=MESH,
        )

    def take(ref, sem):
        pltpu.make_async_copy(ref, ref, sem).wait()

    def load(n):
        part = pl.ds(n * (SLOTS // LOADS), SLOTS // LOADS)
        return pltpu.make_async_copy(tiles_hbm.at[part], tiles.at[part], load_sem.at[n])

    vec_in = pltpu.make_async_copy(vec_hbm, vec, in_sem.at[0])
    pattern_in = pltpu.make_async_copy(pattern_hbm, pattern, in_sem.at[1])
    vec_in.start()
    pattern_in.start()

    barrier = pltpu.get_barrier_semaphore()
    greeted = [(far, col)]
    greeted += [(row, x * 4 + b) for b in z_near]
    greeted += [(row, a * 4 + z) for a in x_near]
    greeted += [(row, x_near[0] * 4 + z_near[1])]
    greeted += [(row, a * 4 + z_near[0]) for a in x_near]
    greeted += [(half * 8 + p, col) for p in pair_ids]
    for to in greeted:
        pl.semaphore_signal(barrier, inc=1, device_id=to, device_id_type=MESH)

    for n in range(LOADS):
        load(n).start()

    vec_in.wait()
    for h in range(2):
        block = vec[pl.ds(h, VEC, stride=2), :]
        now[h] = block
        before[h] = block
        run_m[h, SLOTS] = jnp.zeros((VEC, BS), jnp.float32)
        run_f[h, SLOTS] = jnp.zeros((VEC, HB), jnp.float32)

    def place(par, h):
        block = now[h].astype(jnp.bfloat16)
        yc[h][col] = block
        yr[par, h, row] = block

    def spread(par, h):
        @pl.when(lower)
        def _():
            mine = yr.at[par, h, row]
            remote(mine, mine, yz_send.at[par, h], yz_recv.at[par, h], (far, col)).start()

        mine = yc[h].at[col]
        for n, b in enumerate(z_near):
            remote(mine, mine, cz_send.at[h], cz_recv.at[h, n], (row, x * 4 + b)).start()

        @pl.when(edge)
        def _():
            for a in x_near:
                remote(
                    mine, mine, cx_send.at[h], cx_recv.at[h], (row, a * 4 + z_near[0])
                ).start()

        remote(
            mine, mine, cx_send.at[h], cx_recv.at[h], (row, x_near[0] * 4 + z_near[1])
        ).start()
        for a in x_near:
            remote(mine, mine, cx_send.at[h], cx_recv.at[h], (row, a * 4 + z)).start()
        row_block = yr.at[par, h, row]
        for p in pair_ids:
            remote(
                row_block, row_block, yr_send.at[par, h], yr_recv.at[par, h], (half * 8 + p, col)
            ).start()

    @pl.when(lower)
    def _():
        for r in range(8):
            for par in range(2):
                for h in range(2):
                    yr[par, h, r] = jnp.zeros((VEC, HB), jnp.bfloat16)

    place(0, 0)
    place(0, 1)
    pl.semaphore_wait(barrier, len(greeted))
    spread(0, 0)
    spread(0, 1)

    pattern_in.wait()
    table[...] = jnp.full((8, 128), -1, jnp.int32)
    table[0:2, 0:SLOTS] = pattern[...]
    ids = table[...]
    live = ids >= 0
    keys = jnp.where(live, jnp.concatenate([ids[0:1] % GROUP, ids[1:2] // GROUP, ids[2:8]], axis=0), GROUP)
    down = lax.broadcasted_iota(jnp.int32, (128, 128), 0)
    along = lax.broadcasted_iota(jnp.int32, (128, 128), 1)

    def across(line):
        return jnp.broadcast_to(line, (128, 128))

    row_across, col_across = across(keys[0:1]), across(keys[1:2])
    row_down, col_down = row_across.T, col_across.T

    def count(mask, value=1):
        return jnp.sum(jnp.where(mask, value, 0), axis=0, keepdims=True)

    lines = []
    for key, key_down, source_down in (
        (col_across, col_down, row_down), (row_across, row_down, col_down)
    ):
        rank = count((key_down < key) | ((key_down == key) & (down < along)))
        chosen = across(rank).T == along
        group = count(chosen, key_down)
        lines.append(count(chosen, down))
        lines.append(count(chosen & (source_down < GROUP), source_down))
        lines.append((group != pltpu.roll(group, 1, 1)).astype(jnp.int32))
        lines.append(jnp.where(count(key_down == along) > 0, count(key_down <= along) - 1, SLOTS))
    for n, line in enumerate(lines):
        table[n : n + 1, :] = line
    tell = pltpu.make_async_copy(table, meta, meta_sem)
    tell.start()

    def flip_all():
        for n in range(LOADS):
            load(n).wait()

            def flip(s, carry):
                flipped[s] = tiles[s].T
                return carry

            lax.fori_loop(n * (SLOTS // LOADS), (n + 1) * (SLOTS // LOADS), flip, 0, unroll=True)
        tell.wait()

    def mirror(h):
        total = None
        for p in range(SLOTS):
            s, b = meta[0, p], meta[1, p]
            cut = slice(h * HB, (h + 1) * HB)
            term = jnp.dot(yc[h][b], tiles[s, cut, :], preferred_element_type=jnp.float32)
            total = term if p == 0 else jnp.where(meta[2, p] == 1, term, total + term)
            run_m[h, p] = total

    def forward(h):
        total = None
        for p in range(SLOTS):
            s, b = meta[4, p], meta[5, p]
            cut = slice(h * HB, (h + 1) * HB)
            term = jnp.dot(rows[b], flipped[s, :, cut], preferred_element_type=jnp.float32)
            total = term if p == 0 else jnp.where(meta[6, p] == 1, term, total + term)
            run_f[h, p] = total

    def mirror_block(r):
        last = meta[3, r]
        return (run_m[0, last] + run_m[1, last]).astype(jnp.bfloat16)

    def forward_block(h, c):
        return run_f[h, meta[7, c]].astype(jnp.bfloat16)

    def step(t, carry):
        par = lax.rem(t, 2)

        def pass_on(h, n, near):
            theirs = yc[h].at[x * 4 + z_near[n]]
            take(theirs, cz_recv.at[h, n])
            for a in near:
                remote(theirs, theirs, cx_send.at[h], cx_recv.at[h], (row, a * 4 + z)).start()

        for h in range(2):
            pass_on(h, 2, x_near)

            @pl.when(inner)
            def _():
                pass_on(h, 0, x_near)

            pass_on(h, 1, x_near[1:])

        @pl.when(upper)
        def _():
            for h in range(2):
                theirs = yr.at[par, h, far]
                take(theirs, yz_recv.at[par, h])
                for p in pair_ids:
                    remote(
                        theirs, theirs, yf_send.at[par, h], yf_recv.at[par, h],
                        (half * 8 + p, col),
                    ).start()

        @pl.when(t == 0)
        def _():
            flip_all()

        @pl.when(edge)
        def _():
            for h in range(2):
                pass_on(h, 0, [])

        for h in range(2):
            take(yc[h].at[pl.ds(0, 12)], cx_recv.at[h])
            mirror(h)

        def hand_out(q, base):
            for n, p in enumerate(pair_ids + [pair]):
                block = mirror_block(base + p)
                for h in range(2):
                    piece = block[:, h * HB : (h + 1) * HB]
                    if n < 7:
                        send_m[h, q, n] = piece
                    else:
                        recv_m[par, h, q, pair] = piece
            for h in range(2):
                for n, p in enumerate(pair_ids):
                    remote(
                        send_m.at[h, q, n], recv_m.at[par, h, q, pair],
                        m_send.at[h, q], m_recv.at[par, h, q], (half * 8 + p, col),
                    ).start()

        @pl.when(upper)
        def _():
            hand_out(0, other)

        hand_out(1, half * 8)

        for h in range(2):
            take(yc[h].at[pl.ds(0, 12)], cx_send.at[h])
            take(yc[h].at[pl.ds(0, 3)], cz_send.at[h])
        for h in range(2):
            take(yr.at[par, h, pl.ds(0, 7)], yr_recv.at[par, h])

            @pl.when(upper)
            def _():
                take(yr.at[par, h, pl.ds(0, 7)], yf_recv.at[par, h])

            for r in range(GROUP):
                rows[r, :, h * HB : (h + 1) * HB] = yr[par, h, r]
        for h in range(2):
            forward(h)

            def to_line(n, b, near):
                for m, a in near:
                    send_x[h, n, m] = forward_block(h, a * 4 + b)
                    remote(
                        send_x.at[h, n, m], recv_x.at[h, n, x], x_send.at[h], x_recv.at[h, n],
                        (row, a * 4 + z),
                    ).start()
                recv_x[h, n, x] = forward_block(h, x * 4 + b)

            def to_owner(n, m, dst, sem):
                a, b = x_near[m], z_near[n]
                send_x[h, n, m] = forward_block(h, a * 4 + b)
                remote(
                    send_x.at[h, n, m], dst, x_send.at[h], sem, (row, a * 4 + b)
                ).start()

            numbered = list(enumerate(x_near))

            @pl.when(edge)
            def _():
                for m in range(3):
                    to_owner(0, m, recv_e.at[h, x], e_recv.at[h])
                send_w[h, 0] = forward_block(h, x * 4 + z_near[0])
                remote(
                    send_w.at[h, 0], recv_w.at[h, z], w_send.at[h], w_recv.at[h],
                    (row, x * 4 + z_near[0]),
                ).start()

            to_line(1, z_near[1], numbered[1:])

            @pl.when(inner)
            def _():
                to_line(0, z_near[0], numbered)

            to_line(2, z_near[2], numbered)
            to_owner(1, 0, recv_d.at[h], d_recv.at[h])
            to_line(3, z, numbered)

        def summed(ref, places):
            total = ref[places[0]].astype(jnp.float32)
            for n in places[1:]:
                total = total + ref[n].astype(jnp.float32)
            return total

        @pl.when(upper)
        def _():
            for h in range(2):
                take(recv_m.at[par, h, 0, pl.ds(0, 7)], m_recv.at[par, h, 0])
                send_z[h] = summed(recv_m.at[par, h, 0], range(8)).astype(jnp.bfloat16)
                remote(
                    send_z.at[h], recv_z.at[par, h], z_send.at[h], z_recv.at[par, h], (far, col)
                ).start()

        def line_sum(h, n, places):
            take(recv_x.at[h, n, pl.ds(0, len(places) - 1)], x_recv.at[h, n])
            part = summed(recv_x.at[h, n], places).astype(jnp.bfloat16)
            if n < 3:
                send_w[h, n] = part
                remote(
                    send_w.at[h, n], recv_w.at[h, z], w_send.at[h], w_recv.at[h],
                    (row, x * 4 + z_near[n]),
                ).start()
            else:
                recv_w[h, z] = part

        for h in range(2):
            line_sum(h, 1, [x] + x_near[1:])

            @pl.when(inner)
            def _():
                line_sum(h, 0, range(4))

            line_sum(h, 2, range(4))
            line_sum(h, 3, range(4))
            take(recv_m.at[par, h, 1, pl.ds(0, 7)], m_recv.at[par, h, 1])
            gathered[h] = summed(recv_m.at[par, h, 1], range(8))

        scale = jnp.where(t == 0, 1.0, 2.0).astype(jnp.float32)
        keep = jnp.where(t == 0, 0.0, 1.0).astype(jnp.float32)
        for h in range(2):
            take(recv_d.at[h], d_recv.at[h])
            gathered[h] += recv_d[h].astype(jnp.float32)

            @pl.when(edge)
            def _():
                take(recv_e.at[h, pl.ds(0, 3)], e_recv.at[h])
                gathered[h] += summed(recv_e.at[h], x_near)

            @pl.when(lower)
            def _():
                take(recv_z.at[par, h], z_recv.at[par, h])
                gathered[h] += recv_z[par, h].astype(jnp.float32)

            take(recv_w.at[h, pl.ds(0, 3)], w_recv.at[h])
            total = gathered[h] + summed(recv_w.at[h], range(4))
            present = now[h]
            scaled = (total - CENTER * present) * (1.0 / HALF_WIDTH)
            following = scale * scaled - keep * before[h]
            before[h] = present
            now[h] = following

            @pl.when(t < DEG - 1)
            def _():
                place(1 - par, h)
                spread(1 - par, h)

        for h in range(2):
            take(yr.at[par, h, pl.ds(0, 7)], yr_send.at[par, h])
            take(send_m.at[h, 1], m_send.at[h, 1])
            take(send_x.at[h], x_send.at[h])
            take(send_w.at[h], w_send.at[h])

        @pl.when(upper)
        def _():
            for h in range(2):
                take(yr.at[par, h, pl.ds(0, 7)], yf_send.at[par, h])
                take(send_m.at[h, 0], m_send.at[h, 0])
                take(send_z.at[h], z_send.at[h])

        @pl.when(lower)
        def _():
            for h in range(2):
                take(yr.at[par, h, 0], yz_send.at[par, h])

        return carry

    lax.fori_loop(0, DEG, step, 0)
    for h in range(2):
        out[pl.ds(h, VEC, stride=2), :] = now[h]


def per_device(vectors, tiles, pattern):
    bf16, f32 = jnp.bfloat16, jnp.float32
    dma = pltpu.SemaphoreType.DMA
    vmem = pltpu.VMEM
    filtered = pl.pallas_call(
        kernel,
        out_shape=jax.ShapeDtypeStruct((VEC * 2, HB), f32),
        in_specs=[
            pl.BlockSpec(memory_space=pltpu.HBM),
            pl.BlockSpec(memory_space=pltpu.HBM),
            pl.BlockSpec(memory_space=pltpu.HBM),
        ],
        out_specs=pl.BlockSpec(memory_space=pltpu.VMEM),
        scratch_shapes=[
            vmem((VEC * 2, HB), f32),
            vmem((2, SLOTS), jnp.int32),
            vmem((SLOTS, BS, BS), bf16),
            vmem((SLOTS, BS, BS), bf16),
            vmem((2, SLOTS + 1, VEC, BS), f32),
            vmem((2, SLOTS + 1, VEC, HB), f32),
            vmem((2, VEC, HB), f32),
            vmem((2, VEC, HB), f32),
            vmem((8, 128), jnp.int32),
            pltpu.SMEM((8, 128), jnp.int32),
            vmem((GROUP, VEC, HB), bf16),
            vmem((GROUP, VEC, HB), bf16),
            vmem((2, 2, GROUP, VEC, HB), bf16),
            vmem((GROUP, VEC, BS), bf16),
            vmem((2, 2, 7, VEC, HB), bf16),
            vmem((2, 2, 2, 8, VEC, HB), bf16),
            vmem((2, VEC, HB), bf16),
            vmem((2, 2, VEC, HB), bf16),
            vmem((2, 4, 3, VEC, HB), bf16),
            vmem((2, 4, 4, VEC, HB), bf16),
            vmem((2, 3, VEC, HB), bf16),
            vmem((2, 4, VEC, HB), bf16),
            vmem((2, VEC, HB), bf16),
            vmem((2, 4, VEC, HB), bf16),
            vmem((2, VEC, HB), f32),
            dma((LOADS,)), dma, dma((2,)),
            dma((2,)), dma((2, 3)), dma((2,)), dma((2,)),
            dma((2, 2)), dma((2, 2)), dma((2, 2)), dma((2, 2)), dma((2, 2)), dma((2, 2)),
            dma((2, 2)), dma((2, 2, 2)), dma((2,)), dma((2, 2)),
            dma((2,)), dma((2, 4)), dma((2,)), dma((2,)), dma((2,)), dma((2,)),
        ],
        compiler_params=pltpu.CompilerParams(
            collective_id=0, has_side_effects=True, vmem_limit_bytes=48 * 2**20
        ),
        cost_estimate=pl.CostEstimate(
            flops=DEG * 4 * SLOTS * VEC * BS * BS, bytes_accessed=SLOTS * BS * BS * 2, transcendentals=0
        ),
        name="chebyshev",
    )(vectors.reshape(VEC * 2, HB), pattern[0, 0].T, tiles.reshape(SLOTS, BS, BS))
    return filtered.reshape(VEC, 1, 1, 1, BS)


def solution(mesh):
    placed = (
        P(None, None, "row", "col", None),
        P("row", "col", None, None, None),
        P("row", "col", None, None),
    )
    return jax.shard_map(
        per_device,
        mesh=mesh,
        in_specs=placed,
        out_specs=P(None, None, "row", "col", None),
        check_vma=False,
    )
```

```python
import functools

import jax
import jax.numpy as jnp
from jax import lax
from jax.experimental import pallas as pl
from jax.experimental.pallas import tpu as pltpu
from jax.sharding import PartitionSpec as P

MESH = pl.DeviceIdType.MESH
DEG = 5
CENTER = 0.5
HALF_WIDTH = 3.0
GROUP = 16
SLOTS = 80
VEC = 32
BS = 256
HB = 128
LOADS = 8

PAIR_STEPS = [(dy, dk) for dy in (2, 1, 3, 0) for dk in range(2) if dy or dk]


def kernel(
    vec_hbm, pattern_hbm, tiles_hbm, out,
    vec, pattern,
    tiles, flipped, run_m, run_f, now, before, table, meta,
    yc_0, yc_1, yr, rows, send_m, recv_m, send_z, recv_z, send_x, recv_x, send_w, recv_w, recv_d, recv_e, gathered,
    load_sem, meta_sem, in_sem,
    cz_send, cz_recv, cx_send, cx_recv, yr_send, yr_recv, yz_send, yz_recv, yf_send, yf_recv,
    m_send, m_recv, z_send, z_recv, x_send, x_recv, w_send, w_recv, d_recv, e_recv,
):
    row, col = lax.axis_index("row"), lax.axis_index("col")
    yc = (yc_0, yc_1)
    half = row // 8
    pair = row % 8
    y, core = pair // 2, pair % 2
    x, z = col // 4, col % 4
    other = (1 - half) * 8
    far = other + pair

    z_near = [3 - z, (z + 2) % 4, z + 1 - 2 * (z % 2)]
    edge, inner = z % 3 == 0, z % 3 != 0
    upper, lower = half == 0, half == 1
    x_near = [(x + 2) % 4, (x + 1) % 4, (x + 3) % 4]
    pair_ids = [((y + dy) % 4) * 2 + (core + dk) % 2 for dy, dk in PAIR_STEPS]

    def remote(src, dst, send, recv, to):
        return pltpu.make_async_remote_copy(
            src_ref=src, dst_ref=dst, send_sem=send, recv_sem=recv,
            device_id=to, device_id_type=MESH,
        )

    def take(ref, sem):
        pltpu.make_async_copy(ref, ref, sem).wait()

    def load(n):
        part = pl.ds(n * (SLOTS // LOADS), SLOTS // LOADS)
        return pltpu.make_async_copy(tiles_hbm.at[part], tiles.at[part], load_sem.at[n])

    vec_in = pltpu.make_async_copy(vec_hbm, vec, in_sem.at[0])
    pattern_in = pltpu.make_async_copy(pattern_hbm, pattern, in_sem.at[1])
    vec_in.start()
    pattern_in.start()

    barrier = pltpu.get_barrier_semaphore()
    greeted = [(far, col)]
    greeted += [(row, x * 4 + b) for b in z_near]
    greeted += [(row, a * 4 + z) for a in x_near]
    greeted += [(row, x_near[0] * 4 + z_near[1])]
    greeted += [(row, a * 4 + z_near[0]) for a in x_near]
    greeted += [(half * 8 + p, col) for p in pair_ids]
    for to in greeted:
        pl.semaphore_signal(barrier, inc=1, device_id=to, device_id_type=MESH)

    for n in range(LOADS):
        load(n).start()

    vec_in.wait()
    for h in range(2):
        block = vec[pl.ds(h, VEC, stride=2), :]
        now[h] = block
        before[h] = block
        run_m[h, SLOTS] = jnp.zeros((VEC, BS), jnp.float32)
        run_f[h, SLOTS] = jnp.zeros((VEC, HB), jnp.float32)

    def place(par, h):
        block = now[h].astype(jnp.bfloat16)
        yc[h][col] = block
        yr[par, h, row] = block

    def spread(par, h):
        @pl.when(lower)
        def _():
            mine = yr.at[par, h, row]
            remote(mine, mine, yz_send.at[par, h], yz_recv.at[par, h], (far, col)).start()

        mine = yc[h].at[col]
        for n, b in enumerate(z_near):
            remote(mine, mine, cz_send.at[h], cz_recv.at[h, n], (row, x * 4 + b)).start()

        @pl.when(edge)
        def _():
            for a in x_near:
                remote(
                    mine, mine, cx_send.at[h], cx_recv.at[h], (row, a * 4 + z_near[0])
                ).start()

        remote(
            mine, mine, cx_send.at[h], cx_recv.at[h], (row, x_near[0] * 4 + z_near[1])
        ).start()
        for a in x_near:
            remote(mine, mine, cx_send.at[h], cx_recv.at[h], (row, a * 4 + z)).start()
        row_block = yr.at[par, h, row]
        for p in pair_ids:
            remote(
                row_block, row_block, yr_send.at[par, h], yr_recv.at[par, h], (half * 8 + p, col)
            ).start()

    @pl.when(lower)
    def _():
        for r in range(8):
            for par in range(2):
                for h in range(2):
                    yr[par, h, r] = jnp.zeros((VEC, HB), jnp.bfloat16)

    place(0, 0)
    place(0, 1)

    pattern_in.wait()
    table[...] = jnp.full((8, 128), -1, jnp.int32)
    table[0:2, 0:SLOTS] = pattern[...]
    ids = table[...]
    live = ids >= 0
    keys = jnp.where(live, jnp.concatenate([ids[0:1] % GROUP, ids[1:2] // GROUP, ids[2:8]], axis=0), GROUP)
    down = lax.broadcasted_iota(jnp.int32, (128, 128), 0)
    along = lax.broadcasted_iota(jnp.int32, (128, 128), 1)

    def across(line):
        return jnp.broadcast_to(line, (128, 128))

    row_across, col_across = across(keys[0:1]), across(keys[1:2])
    row_down, col_down = row_across.T, col_across.T

    def count(mask, value=1):
        return jnp.sum(jnp.where(mask, value, 0), axis=0, keepdims=True)

    lines = []
    for key, key_down, source_down in (
        (col_across, col_down, row_down), (row_across, row_down, col_down)
    ):
        rank = count((key_down < key) | ((key_down == key) & (down < along)))
        chosen = across(rank).T == along
        group = count(chosen, key_down)
        lines.append(count(chosen, down))
        lines.append(count(chosen & (source_down < GROUP), source_down))
        lines.append((group != pltpu.roll(group, 1, 1)).astype(jnp.int32))
        lines.append(jnp.where(count(key_down == along) > 0, count(key_down <= along) - 1, SLOTS))
    for n, line in enumerate(lines):
        table[n : n + 1, :] = line
    tell = pltpu.make_async_copy(table, meta, meta_sem)
    tell.start()

    def flip_part(parts):
        for n in parts:
            load(n).wait()

            def flip(s, carry):
                flipped[s] = tiles[s].T
                return carry

            lax.fori_loop(n * (SLOTS // LOADS), (n + 1) * (SLOTS // LOADS), flip, 0, unroll=True)

    flip_part(range(2))
    pl.semaphore_wait(barrier, len(greeted))
    spread(0, 0)
    spread(0, 1)

    def flip_all():
        flip_part(range(2, LOADS))
        tell.wait()

    def mirror(h):
        total = None
        for p in range(SLOTS):
            s, b = meta[0, p], meta[1, p]
            cut = slice(h * HB, (h + 1) * HB)
            term = jnp.dot(yc[h][b], tiles[s, cut, :], preferred_element_type=jnp.float32)
            total = term if p == 0 else jnp.where(meta[2, p] == 1, term, total + term)
            run_m[h, p] = total

    def forward(h):
        total = None
        for p in range(SLOTS):
            s, b = meta[4, p], meta[5, p]
            cut = slice(h * HB, (h + 1) * HB)
            term = jnp.dot(rows[b], flipped[s, :, cut], preferred_element_type=jnp.float32)
            total = term if p == 0 else jnp.where(meta[6, p] == 1, term, total + term)
            run_f[h, p] = total

    def mirror_block(r):
        last = meta[3, r]
        return (run_m[0, last] + run_m[1, last]).astype(jnp.bfloat16)

    def forward_block(h, c):
        return run_f[h, meta[7, c]].astype(jnp.bfloat16)

    def step(t, carry):
        par = lax.rem(t, 2)

        def pass_on(h, n, near):
            theirs = yc[h].at[x * 4 + z_near[n]]
            take(theirs, cz_recv.at[h, n])
            for a in near:
                remote(theirs, theirs, cx_send.at[h], cx_recv.at[h], (row, a * 4 + z)).start()

        for h in range(2):
            pass_on(h, 2, x_near)

            @pl.when(inner)
            def _():
                pass_on(h, 0, x_near)

            pass_on(h, 1, x_near[1:])

        @pl.when(upper)
        def _():
            for h in range(2):
                theirs = yr.at[par, h, far]
                take(theirs, yz_recv.at[par, h])
                for p in pair_ids:
                    remote(
                        theirs, theirs, yf_send.at[par, h], yf_recv.at[par, h],
                        (half * 8 + p, col),
                    ).start()

        @pl.when(t == 0)
        def _():
            flip_all()

        @pl.when(edge)
        def _():
            for h in range(2):
                pass_on(h, 0, [])

        for h in range(2):
            take(yc[h].at[pl.ds(0, 12)], cx_recv.at[h])
            mirror(h)

        def hand_out(q, base):
            for n, p in enumerate(pair_ids + [pair]):
                block = mirror_block(base + p)
                for h in range(2):
                    piece = block[:, h * HB : (h + 1) * HB]
                    if n < 7:
                        send_m[h, q, n] = piece
                    else:
                        recv_m[par, h, q, pair] = piece
            for h in range(2):
                for n, p in enumerate(pair_ids):
                    remote(
                        send_m.at[h, q, n], recv_m.at[par, h, q, pair],
                        m_send.at[h, q], m_recv.at[par, h, q], (half * 8 + p, col),
                    ).start()

        @pl.when(upper)
        def _():
            hand_out(0, other)

        hand_out(1, half * 8)

        for h in range(2):
            take(yc[h].at[pl.ds(0, 12)], cx_send.at[h])
            take(yc[h].at[pl.ds(0, 3)], cz_send.at[h])
        for h in range(2):
            take(yr.at[par, h, pl.ds(0, 7)], yr_recv.at[par, h])

            @pl.when(upper)
            def _():
                take(yr.at[par, h, pl.ds(0, 7)], yf_recv.at[par, h])

            for r in range(GROUP):
                rows[r, :, h * HB : (h + 1) * HB] = yr[par, h, r]
        for h in range(2):
            forward(h)

            def to_line(n, b, near):
                for m, a in near:
                    send_x[h, n, m] = forward_block(h, a * 4 + b)
                    remote(
                        send_x.at[h, n, m], recv_x.at[h, n, x], x_send.at[h], x_recv.at[h, n],
                        (row, a * 4 + z),
                    ).start()
                recv_x[h, n, x] = forward_block(h, x * 4 + b)

            def to_owner(n, m, dst, sem):
                a, b = x_near[m], z_near[n]
                send_x[h, n, m] = forward_block(h, a * 4 + b)
                remote(
                    send_x.at[h, n, m], dst, x_send.at[h], sem, (row, a * 4 + b)
                ).start()

            numbered = list(enumerate(x_near))

            @pl.when(edge)
            def _():
                for m in range(3):
                    to_owner(0, m, recv_e.at[h, x], e_recv.at[h])
                send_w[h, 0] = forward_block(h, x * 4 + z_near[0])
                remote(
                    send_w.at[h, 0], recv_w.at[h, z], w_send.at[h], w_recv.at[h],
                    (row, x * 4 + z_near[0]),
                ).start()

            to_line(1, z_near[1], numbered[1:])

            @pl.when(inner)
            def _():
                to_line(0, z_near[0], numbered)

            to_line(2, z_near[2], numbered)
            to_owner(1, 0, recv_d.at[h], d_recv.at[h])
            to_line(3, z, numbered)

        def summed(ref, places):
            total = ref[places[0]].astype(jnp.float32)
            for n in places[1:]:
                total = total + ref[n].astype(jnp.float32)
            return total

        @pl.when(upper)
        def _():
            for h in range(2):
                take(recv_m.at[par, h, 0, pl.ds(0, 7)], m_recv.at[par, h, 0])
                send_z[h] = summed(recv_m.at[par, h, 0], range(8)).astype(jnp.bfloat16)
                remote(
                    send_z.at[h], recv_z.at[par, h], z_send.at[h], z_recv.at[par, h], (far, col)
                ).start()

        def line_sum(h, n, places):
            take(recv_x.at[h, n, pl.ds(0, len(places) - 1)], x_recv.at[h, n])
            part = summed(recv_x.at[h, n], places).astype(jnp.bfloat16)
            if n < 3:
                send_w[h, n] = part
                remote(
                    send_w.at[h, n], recv_w.at[h, z], w_send.at[h], w_recv.at[h],
                    (row, x * 4 + z_near[n]),
                ).start()
            else:
                recv_w[h, z] = part

        for h in range(2):
            line_sum(h, 1, [x] + x_near[1:])

            @pl.when(inner)
            def _():
                line_sum(h, 0, range(4))

            line_sum(h, 2, range(4))
            line_sum(h, 3, range(4))

        for h in range(2):
            take(recv_m.at[par, h, 1, pl.ds(0, 7)], m_recv.at[par, h, 1])
            gathered[h] = summed(recv_m.at[par, h, 1], range(8))

        scale = jnp.where(t == 0, 1.0, 2.0).astype(jnp.float32)
        keep = jnp.where(t == 0, 0.0, 1.0).astype(jnp.float32)
        for h in range(2):
            take(recv_d.at[h], d_recv.at[h])
            gathered[h] += recv_d[h].astype(jnp.float32)

            @pl.when(edge)
            def _():
                take(recv_e.at[h, pl.ds(0, 3)], e_recv.at[h])
                gathered[h] += summed(recv_e.at[h], x_near)

            @pl.when(lower)
            def _():
                take(recv_z.at[par, h], z_recv.at[par, h])
                gathered[h] += recv_z[par, h].astype(jnp.float32)

            take(recv_w.at[h, pl.ds(0, 3)], w_recv.at[h])
            total = gathered[h] + summed(recv_w.at[h], range(4))
            present = now[h]
            scaled = (total - CENTER * present) * (1.0 / HALF_WIDTH)
            following = scale * scaled - keep * before[h]
            before[h] = present
            now[h] = following

            @pl.when(t < DEG - 1)
            def _():
                place(1 - par, h)
                spread(1 - par, h)

        for h in range(2):
            take(yr.at[par, h, pl.ds(0, 7)], yr_send.at[par, h])
            take(send_m.at[h, 1], m_send.at[h, 1])
            take(send_x.at[h], x_send.at[h])
            take(send_w.at[h], w_send.at[h])

        @pl.when(upper)
        def _():
            for h in range(2):
                take(yr.at[par, h, pl.ds(0, 7)], yf_send.at[par, h])
                take(send_m.at[h, 0], m_send.at[h, 0])
                take(send_z.at[h], z_send.at[h])

        @pl.when(lower)
        def _():
            for h in range(2):
                take(yr.at[par, h, 0], yz_send.at[par, h])

        return carry

    lax.fori_loop(0, DEG, step, 0)
    for h in range(2):
        out[pl.ds(h, VEC, stride=2), :] = now[h]


def per_device(vectors, tiles, pattern):
    bf16, f32 = jnp.bfloat16, jnp.float32
    dma = pltpu.SemaphoreType.DMA
    vmem = pltpu.VMEM
    filtered = pl.pallas_call(
        kernel,
        out_shape=jax.ShapeDtypeStruct((VEC * 2, HB), f32),
        in_specs=[
            pl.BlockSpec(memory_space=pltpu.HBM),
            pl.BlockSpec(memory_space=pltpu.HBM),
            pl.BlockSpec(memory_space=pltpu.HBM),
        ],
        out_specs=pl.BlockSpec(memory_space=pltpu.VMEM),
        scratch_shapes=[
            vmem((VEC * 2, HB), f32),
            vmem((2, SLOTS), jnp.int32),
            vmem((SLOTS, BS, BS), bf16),
            vmem((SLOTS, BS, BS), bf16),
            vmem((2, SLOTS + 1, VEC, BS), f32),
            vmem((2, SLOTS + 1, VEC, HB), f32),
            vmem((2, VEC, HB), f32),
            vmem((2, VEC, HB), f32),
            vmem((8, 128), jnp.int32),
            pltpu.SMEM((8, 128), jnp.int32),
            vmem((GROUP, VEC, HB), bf16),
            vmem((GROUP, VEC, HB), bf16),
            vmem((2, 2, GROUP, VEC, HB), bf16),
            vmem((GROUP, VEC, BS), bf16),
            vmem((2, 2, 7, VEC, HB), bf16),
            vmem((2, 2, 2, 8, VEC, HB), bf16),
            vmem((2, VEC, HB), bf16),
            vmem((2, 2, VEC, HB), bf16),
            vmem((2, 4, 3, VEC, HB), bf16),
            vmem((2, 4, 4, VEC, HB), bf16),
            vmem((2, 3, VEC, HB), bf16),
            vmem((2, 4, VEC, HB), bf16),
            vmem((2, VEC, HB), bf16),
            vmem((2, 4, VEC, HB), bf16),
            vmem((2, VEC, HB), f32),
            dma((LOADS,)), dma, dma((2,)),
            dma((2,)), dma((2, 3)), dma((2,)), dma((2,)),
            dma((2, 2)), dma((2, 2)), dma((2, 2)), dma((2, 2)), dma((2, 2)), dma((2, 2)),
            dma((2, 2)), dma((2, 2, 2)), dma((2,)), dma((2, 2)),
            dma((2,)), dma((2, 4)), dma((2,)), dma((2,)), dma((2,)), dma((2,)),
        ],
        compiler_params=pltpu.CompilerParams(
            collective_id=0, has_side_effects=True, vmem_limit_bytes=63 * 2**20
        ),
        cost_estimate=pl.CostEstimate(
            flops=DEG * 4 * SLOTS * VEC * BS * BS, bytes_accessed=SLOTS * BS * BS * 2, transcendentals=0
        ),
        name="chebyshev",
    )(vectors.reshape(VEC * 2, HB), pattern[0, 0].T, tiles.reshape(SLOTS, BS, BS))
    return filtered.reshape(VEC, 1, 1, 1, BS)


def solution(mesh):
    placed = (
        P(None, None, "row", "col", None),
        P("row", "col", None, None, None),
        P("row", "col", None, None),
    )
    return jax.shard_map(
        per_device,
        mesh=mesh,
        in_specs=placed,
        out_specs=P(None, None, "row", "col", None),
        check_vma=False,
    )
```
